32 devices in a mesh: space: 16 (over z, y, x), dp: 2 (over core).
Axes of the slice: x: 2, y: 2, z: 4, core: 2. Of those that a mesh axis runs over, the one named last changes fastest.
Arguments:
- features: bfloat16 [192, 8, 8, 512], P(('space', 'dp')), may hold values from -6 to 6
- grad_out: bfloat16 [192, 8, 8, 512], P(('space', 'dp')), may hold values from -6 to 6
- occupancy: int32 [192, 512], P(('space', 'dp')), may hold values 0 or 1
- weight: bfloat16 [3, 3, 3, 64, 64], replicated, may hold values from -0.15625 to 0.15625
- neighbours: int32 [192, 26], P(('space', 'dp')), may hold values from 0 to 14, as said below
- send_rows: int32 [32, 4, 2], P(('space', 'dp')), may hold values from 0 to 6, as said below
Outputs:
- output: bfloat16 [192, 8, 8, 512], P(('space', 'dp'))
- feature_grad: bfloat16 [192, 8, 8, 512], P(('space', 'dp'))
- weight_grad: float32 [3, 3, 3, 64, 64], replicated
The draws below stay inside these ranges and needn't reach their ends.
Inputs may be any that keep to these rules, and one draw needn't show every extreme that they name: `neighbours`: A value below 6 names another block of the same device; 6 + k * 2 + j names slot j of list k of the device k sends from, that is the device 1 lower, 1 higher, 2 lower, 2 higher along space for k = 0, 1, 2, 3 (same dp index); 14 names no block. Every filled slot of a list sent to a device is named by some entry of that device, and no unfilled slot is named. `send_rows`: list k of a device holds the blocks it sends to the device 1 higher, 1 lower, 2 higher, 2 lower along space for k = 0, 1, 2, 3 (same dp index); 6 marks an unfilled slot, filled slots come first and name distinct blocks; lists to devices outside the axis are unfilled.
All inputs are finite; a program needn't handle non-finite values. No bound on the sum of `occupancy` on one device may be relied on, other than what follows from the above.
Results may differ from the reference program's by a relative error of at most 0.003.
Values may be sent and summed in bfloat16 or wider, within the bound.
A program may use at most 128 MiB of HBM per device.

```python
import math
import jax
import jax.numpy as jnp
from jax import lax

EDGE = 8
C = 64
B_DEV = 6
CAP = 2
RANKS = 16
GROUPS = 32
BLOCKS = 192
N_SPACE = 16
N_DP = 2


def plan_tables(key):
    base_key = jax.random.fold_in(key, 11)
    subkeys = jax.random.split(base_key, 6)
    groups = GROUPS
    blocks = B_DEV
    slot_count = CAP
    layers = groups // RANKS
    distances = jnp.array([1, -1, 2, -2], jnp.int32)
    device = jnp.arange(groups, dtype=jnp.int32)
    position = device // layers
    counts = jax.random.randint(subkeys[0], (groups, 4), (slot_count + 1) // 2, slot_count + 1)
    counts = counts.at[:, 0].set(slot_count)
    source = position[:, None] - distances[None, :]
    from_ok = (source >= 0) & (source < RANKS)
    target = position[:, None] + distances[None, :]
    to_ok = (target >= 0) & (target < RANKS)
    target_dev = jnp.clip(device[:, None] + distances[None, :] * layers, 0, groups - 1)
    target_count = counts[target_dev, jnp.arange(4)[None, :]]
    perm_keys = jax.random.split(subkeys[1], groups * 4)
    orders = jax.vmap(lambda subkey: jax.random.permutation(subkey, blocks))(perm_keys).reshape(groups, 4, blocks)[:, :, :slot_count]
    slot_ids = jnp.arange(slot_count)
    send_table = jnp.where(to_ok[:, :, None] & (slot_ids[None, None, :] < target_count[:, :, None]), orders, blocks)
    grid_shape = (groups, blocks, 26)
    kind_draw = jax.random.randint(subkeys[2], grid_shape, 0, 4)
    local_row = (jnp.arange(blocks)[None, :, None] + 1 + jax.random.randint(subkeys[3], grid_shape, 0, max(blocks - 1, 1))) % blocks
    peer_pick = jax.random.randint(subkeys[4], grid_shape, 0, 4)
    peer_count = counts[device[:, None, None], peer_pick]
    slot_pick = jax.random.randint(subkeys[5], grid_shape, 0, slot_count) % peer_count
    peer_ok = from_ok[device[:, None, None], peer_pick]
    remote = blocks + peer_pick * slot_count + slot_pick
    empty_row = blocks + 4 * slot_count
    beside = jnp.where(kind_draw == 0, empty_row, jnp.where((kind_draw == 1) & peer_ok, remote, local_row))
    all_slots = jnp.arange(4 * slot_count)
    slot_peer = all_slots // slot_count
    slot_place = all_slots % slot_count
    needed = from_ok[:, slot_peer] & (slot_place[None, :] < counts[:, slot_peer])
    fix_row = all_slots % blocks
    column = 25 - all_slots // blocks
    current = beside[:, fix_row, column]
    beside = beside.at[:, fix_row, column].set(jnp.where(needed, blocks + all_slots[None, :], current))
    return (beside.reshape(groups * blocks, 26).astype(jnp.int32), send_table.astype(jnp.int32))


def draw_neighbours(key, part):
    return plan_tables(key)[0]


def draw_send_rows(key, part):
    return plan_tables(key)[1]


def plant(values, rng, least, top_value):
    shape = values.shape
    index_at = [jax.random.randint(jax.random.fold_in(rng, axis), (), 0, shape[axis]) for axis in range(len(shape))]
    values = values.at[tuple(index_at)].set(least)
    longest = shape.index(max(shape))
    index_at[longest] = (index_at[longest] + 1) % shape[longest]
    return values.at[tuple(index_at)].set(top_value)


def steps_of(own_key, shape, shards, smallest, top_value):
    factor_of = 1.0
    for dim, blocks in shards:
        steps = jax.random.uniform(jax.random.fold_in(jax.random.fold_in(own_key, 6), dim), (blocks,), jnp.float32, smallest / len(shards), top_value / len(shards))
        factor_of = factor_of * jnp.repeat(jnp.exp(steps), shape[dim] // blocks).reshape((-1,) + (1,) * (len(shape) - 1 - dim))
    return factor_of


def centred(rng, extent, spread, bound, cuts=(), kind=jnp.bfloat16):
    factor_of = steps_of(rng, extent, cuts, -0.22, 0.18) if cuts else 1.0
    values = jax.random.normal(rng, extent, jnp.float32) * spread * factor_of
    return jnp.minimum(jnp.maximum(values, -bound), bound).astype(kind)


def setup_inputs(seed: int = 0) -> dict:
    key_list = jax.random.split(jax.random.key(seed), 7)
    return {
        "features": centred(key_list[0], (BLOCKS, EDGE, EDGE, EDGE * C), 1.0, 6.0, ((0, 32),)),
        "grad_out": centred(key_list[1], (BLOCKS, EDGE, EDGE, EDGE * C), 1.0, 6.0, ((0, 32),)),
        "occupancy": plant((jax.random.randint(key_list[2], (BLOCKS, EDGE ** 3), 0, 3) < 2).astype(jnp.int32), jax.random.fold_in(key_list[2], 1), 0, 1),
        "weight": centred(key_list[3], (3, 3, 3, C, C), (27 * C) ** -0.5, 0.15625),
        "neighbours": draw_neighbours(jax.random.fold_in(key_list[6], 71), 0),
        "send_rows": draw_send_rows(jax.random.fold_in(key_list[6], 71), 0),
    }


DISTANCES = (1, -1, 2, -2)
OFFSETS = [(step_x, step_y, step_z) for step_x in (-1, 0, 1) for step_y in (-1, 0, 1) for step_z in (-1, 0, 1) if (step_x, step_y, step_z) != (0, 0, 0)]
REACH = {-1: (7, 8, 0, 1), 0: (0, 8, 1, 9), 1: (0, 1, 9, 10)}

def matmul(left, right, left_dim, right_dim):
    dims = (((left_dim,), (right_dim,)), ((), ()))
    return lax.dot_general(left.astype(jnp.float32), right.astype(jnp.float32), dims, precision=lax.Precision.HIGHEST, preferred_element_type=jnp.float32)

def expand_mask(occupancy, channels):
    block_count = occupancy.shape[0]
    return jnp.repeat(occupancy.reshape(block_count, 8, 8, 8), channels, axis=3)

def band_weights(weight):
    channels = weight.shape[-1]
    zero_block = jnp.zeros((3, 3, channels, channels), weight.dtype)
    stacked = []
    for tap_in in range(4):
        parts = [weight[:, :, tap_in - out_pos] if 0 <= tap_in - out_pos <= 2 else zero_block for out_pos in range(2)]
        stacked.append(jnp.concatenate(parts, axis=3))
    return jnp.concatenate(stacked, axis=2)

def window_rows(slab, channels):
    block_count = slab.shape[0]
    stacked = jnp.stack([slab[..., 2 * channels * pair_num:2 * channels * pair_num + 4 * channels] for pair_num in range(4)], axis=3)
    return stacked.reshape(block_count * 256, 4 * channels)

def face_regions(table, channels):
    regions = []
    for step_x, step_y, step_z in OFFSETS:
        x_low, x_high = REACH[step_x][:2]
        y_low, y_high = REACH[step_y][:2]
        z_low, z_high = REACH[step_z][:2]
        regions.append(table[:, x_low:x_high, y_low:y_high, z_low * channels:z_high * channels])
    return regions

def assemble(regions, centre, index):
    pieces = {(0, 0, 0): centre}
    for slot_num, offset in enumerate(OFFSETS):
        pieces[offset] = jnp.take(regions[slot_num], index[:, slot_num], axis=0)
    planes = []
    for step_x in (-1, 0, 1):
        lines = []
        for step_y in (-1, 0, 1):
            lines.append(jnp.concatenate([pieces[step_x, step_y, step_z] for step_z in (-1, 0, 1)], axis=3))
        planes.append(jnp.concatenate(lines, axis=2))
    return jnp.concatenate(planes, axis=1)

def local_passes(padded, live_float, grads, banded):
    channels = banded.shape[-1] // 2
    block_count = padded.shape[0]
    grad_rows = grads.reshape(block_count * 256, 2 * channels)
    total = jnp.zeros((block_count * 256, 2 * channels), jnp.float32)
    dpad = jnp.zeros((block_count, 10, 10, 10 * channels), jnp.float32)
    dband = {}
    for shift_x in range(3):
        for shift_y in range(3):
            rows = window_rows(padded[:, shift_x:shift_x + 8, shift_y:shift_y + 8], channels)
            total = total + matmul(rows, banded[shift_x, shift_y], 1, 0)
            dband[shift_x, shift_y] = matmul(rows, grad_rows, 0, 0)
            back = matmul(grad_rows, banded[shift_x, shift_y], 1, 1).reshape(block_count, 8, 8, 4, 4 * channels)
            dslab = jnp.zeros((block_count, 8, 8, 10 * channels), jnp.float32)
            for pair_num in range(4):
                dslab = dslab.at[..., 2 * channels * pair_num:2 * channels * pair_num + 4 * channels].add(back[:, :, :, pair_num])
            dpad = dpad.at[:, shift_x:shift_x + 8, shift_y:shift_y + 8].add(dslab)
    output = (total.reshape(block_count, 8, 8, 8 * channels) * live_float).astype(jnp.bfloat16)

    def tap(shift_x, shift_y, shift_z):
        full = dband[shift_x, shift_y]
        terms = [full[(out_pos + shift_z) * channels:(out_pos + shift_z + 1) * channels, out_pos * channels:(out_pos + 1) * channels] for out_pos in range(2)]
        return terms[0] + terms[1]
    dweight = jnp.stack([jnp.stack([jnp.stack([tap(shift_x, shift_y, shift_z) for shift_z in range(3)]) for shift_y in range(3)]) for shift_x in range(3)])
    return (output, dpad, dweight)

def reference(features, grad_out, occupancy, weight, neighbours, send_rows):
    channels = weight.shape[-1]
    blocks = B_DEV
    slot_count = CAP
    groups = N_SPACE * N_DP
    live = expand_mask(occupancy, channels) == 1
    shown = jnp.where(live, features, jnp.zeros_like(features))
    masked_grad = jnp.where(live, grad_out, jnp.zeros_like(grad_out))
    live_float = live.astype(jnp.float32)
    table = jnp.concatenate([shown, jnp.zeros((1, 8, 8, 8 * channels), jnp.bfloat16)], axis=0)
    device = jnp.arange(groups, dtype=jnp.int32)
    position = device // N_DP
    distance = jnp.array(DISTANCES, dtype=jnp.int32)
    source_space = position[:, None] - distance[None, :]
    source_ok = (source_space >= 0) & (source_space < N_SPACE)
    source_dev = jnp.clip(device[:, None] - distance[None, :] * N_DP, 0, groups - 1).astype(jnp.int32)
    sent = send_rows[source_dev, jnp.arange(4, dtype=jnp.int32)[None, :]]
    recv_global = jnp.where(source_ok[:, :, None] & (sent < blocks), source_dev[:, :, None] * blocks + sent, BLOCKS)
    recv_flat = recv_global.reshape(groups, 4 * slot_count).astype(jnp.int32)
    local_ids = neighbours.reshape(groups, blocks, 26)
    remote_pos = jnp.clip(local_ids - blocks, 0, 4 * slot_count - 1).astype(jnp.int32)
    remote_ids = recv_flat[device[:, None, None], remote_pos]
    global_ids = jnp.where(local_ids < blocks, device[:, None, None] * blocks + local_ids, jnp.where(local_ids == blocks + 4 * slot_count, BLOCKS, remote_ids)).astype(jnp.int32)
    regions = face_regions(table, channels)
    banded = band_weights(weight)

    def step(carry, device_num):
        accum, dsum = carry
        start = (device_num * blocks).astype(jnp.int32)
        centre = lax.dynamic_slice_in_dim(shown, start, blocks, 0)
        index = lax.dynamic_index_in_dim(global_ids, device_num, 0, keepdims=False)
        grads = lax.dynamic_slice_in_dim(masked_grad, start, blocks, 0)
        live_here = lax.dynamic_slice_in_dim(live_float, start, blocks, 0)
        padded = assemble(regions, centre, index)
        output, dpad, dweight = local_passes(padded, live_here, grads, banded)
        inner = dpad[:, 1:9, 1:9, channels:9 * channels]
        accum = lax.dynamic_update_slice_in_dim(accum, lax.dynamic_slice_in_dim(accum, start, blocks, 0) + inner, start, 0)
        for slot_num, offset in enumerate(OFFSETS):
            xn0, xn1, xp0, xp1 = REACH[offset[0]]
            yn0, yn1, yp0, yp1 = REACH[offset[1]]
            zn0, zn1, zp0, zp1 = REACH[offset[2]]
            accum = accum.at[index[:, slot_num], xn0:xn1, yn0:yn1, zn0 * channels:zn1 * channels].add(dpad[:, xp0:xp1, yp0:yp1, zp0 * channels:zp1 * channels])
        return ((accum, dsum + dweight), output)
    init = (jnp.zeros((BLOCKS + 1, 8, 8, 8 * channels), jnp.float32), jnp.zeros((3, 3, 3, channels, channels), jnp.float32))
    (accum, dsum), outputs = lax.scan(step, init, jnp.arange(groups, dtype=jnp.int32))
    output = outputs.reshape(BLOCKS, 8, 8, 8 * channels)
    feature_grad = (accum[:BLOCKS] * live_float).astype(jnp.bfloat16)
    weight_grad = dsum * (1.0 / math.sqrt(BLOCKS * 512))
    return (output, feature_grad, weight_grad)
```

```python
import functools
import math

import jax
import jax.numpy as jnp
from jax import lax
from jax.experimental import pallas as pl
from jax.experimental.pallas import tpu as pltpu
from jax.sharding import PartitionSpec as P

DISTANCES = (1, -1, 2, -2)
OFFSETS = [
    (step_x, step_y, step_z)
    for step_x in (-1, 0, 1)
    for step_y in (-1, 0, 1)
    for step_z in (-1, 0, 1)
    if (step_x, step_y, step_z) != (0, 0, 0)
]
SLOT = {offset: num for num, offset in enumerate(OFFSETS)}
PLANES = {-1: (7, 8, 0, 1), 0: (0, 8, 1, 9), 1: (0, 1, 9, 10)}
F32, BF16 = jnp.float32, jnp.bfloat16
VMEM = pl.BlockSpec(memory_space=pltpu.VMEM)
SMEM = pl.BlockSpec(memory_space=pltpu.SMEM)
LIMIT = 56 * 1024 * 1024


def shifted(block, axis, distance):
    devices = range(lax.axis_size(axis))
    route = [(i - distance, i) for i in devices if i - distance in devices]
    return lax.ppermute(block, axis, route)


def band_weights(weight):
    channels = weight.shape[-1]
    zero_block = jnp.zeros((3, 3, channels, channels), weight.dtype)
    stacked = []
    for tap_in in range(4):
        parts = [
            weight[:, :, tap_in - out_pos] if 0 <= tap_in - out_pos <= 2 else zero_block
            for out_pos in range(2)
        ]
        stacked.append(jnp.concatenate(parts, axis=3))
    return jnp.stack(stacked, axis=2)


def live_mask(occ):
    spread = (
        lax.broadcasted_iota(jnp.int32, (8, 512), 1) // 64
        == lax.broadcasted_iota(jnp.int32, (8, 512), 0)
    ).astype(BF16)
    return jnp.dot(occ, spread, preferred_element_type=F32).reshape(8, 8, 512)


def mask_feats(mask, values):
    return jnp.where(mask > 0.5, values.astype(F32), 0.0)


def outgoing_kernel(feat, occ, send, out):
    nb, cap = feat.shape[0], send.shape[2]
    for k in range(4):
        for j in range(cap):
            row = jnp.minimum(send[0, k, j], nb - 1)
            out[k, j] = mask_feats(live_mask(occ[row]), feat[row]).astype(BF16)


def build_bands(band, bands):
    zero = jnp.zeros((64, 128), BF16)
    for a in range(3):
        for c in range(3):
            for k, r in enumerate((0, 1, 2, 3, 4, None, None, -1)):
                for j in range(2):
                    d = None if r is None else r - 2 * j
                    piece = zero if d is None or not -1 <= d <= 2 else band[a, c, d + 1]
                    bands[c, 64 * k : 64 * k + 64, 256 * a + 128 * j : 256 * a + 128 * j + 128] = piece


def pair_store(dst, lead, row0, tiles, lanes):
    for b in range(0, len(tiles), 2):
        both = jnp.concatenate([tiles[b], tiles[b + 1]], axis=0).astype(BF16)
        if lead is None:
            dst[row0 + 8 * b : row0 + 8 * b + 16, lanes] = both
        else:
            dst[lead, row0 + 8 * b : row0 + 8 * b + 16, lanes] = both


def fill_grads(nb, grad, mask, gz, gt):
    wide = 8 * nb
    for x in (0, 1, 10, 11):
        gz[x * wide : (x + 1) * wide] = jnp.zeros((wide, 512), BF16)
    for b in range(0, nb, 2):
        one = mask_feats(mask[b], grad[b])
        two = mask_feats(mask[b + 1], grad[b + 1])
        both = jnp.concatenate([one, two], axis=1).astype(BF16)
        for x in range(8):
            row = (x + 2) * wide + 8 * b
            gz[row : row + 16] = both[x]
    flat = gz[2 * wide : 10 * wide].astype(F32).T.astype(BF16)
    gt[:, : 8 * wide] = flat[:256]
    gt[:, 8 * wide :] = flat[256:]


def nt_dot(left, right):
    return lax.dot_general(left, right, (((1,), (1,)), ((), ())), preferred_element_type=F32)


def back_matmuls(nb, gz, bands, dp):
    wide = 8 * nb
    for c in range(3):
        parts = []
        for w in range(2):
            left = jnp.concatenate(
                [gz[wide * (2 - a) : wide * (12 - a), 256 * w : 256 * w + 256] for a in range(3)],
                axis=1,
            )
            parts.append(nt_dot(left, bands[c]).reshape(10, nb, 8, 512))
        one, two = parts
        dp[c, :, :, :, 0:128] = one[..., 0:128]
        dp[c, :, :, :, 128:256] = one[..., 128:256] + two[..., 384:512]
        dp[c, :, :, :, 256:384] = one[..., 256:384] + two[..., 0:128]
        dp[c, :, :, :, 384:512] = two[..., 128:256]
        dp[c, :, :, :, 512:640] = one[..., 384:512] + two[..., 256:384]


def scatter(nb, dp, nbr, acc):
    acc[...] = jnp.zeros(acc.shape, F32)
    for b in range(nb):
        for ox in (0, -1, 1):
            x0, x1, p0, p1 = PLANES[ox]
            n = p1 - p0
            row = lax.broadcasted_iota(jnp.int32, (n, 8, 640), 1)
            low = lax.broadcasted_iota(jnp.int32, (n, 8, 128), 2) < 64
            flat = (n * 8, 640)

            def turned(value, by):
                return pltpu.roll(value, by, 1)

            r0 = turned(dp[0, p0:p1, b], 7)
            r2 = turned(dp[2, p0:p1, b], 1)
            tiles = {
                0: dp[1, p0:p1, b] + jnp.where(row < 7, r0, 0.0) + jnp.where(row > 0, r2, 0.0),
                -1: jnp.where(row == 7, r0, 0.0),
                1: jnp.where(row == 0, r2, 0.0),
            }
            for oy in (0, -1, 1):
                tile = tiles[oy]
                t = b if (ox, oy) == (0, 0) else nbr[b, SLOT[ox, oy, 0]]
                acc[t, x0:x1] += tile[..., :512]
                halo = tile[..., 512:]
                acc[nbr[b, SLOT[ox, oy, 1]], x0:x1, :, 0:128] += jnp.where(low, halo, 0.0)
                acc[nbr[b, SLOT[ox, oy, -1]], x0:x1, :, 384:512] += jnp.where(low, 0.0, halo)


def fill_padded(nb, table, nbr, pad):
    row = lax.broadcasted_iota(jnp.int32, (8, 640), 0)
    low = lax.broadcasted_iota(jnp.int32, (8, 128), 1) < 64
    for xp in range(10):
        ox = -1 if xp == 0 else 1 if xp == 9 else 0
        xs = {-1: 7, 0: xp - 1, 1: 0}[ox]
        shifts = ([], [], [])
        for b in range(nb):

            def tile(oy):
                t = b if (ox, oy) == (0, 0) else nbr[b, SLOT[ox, oy, 0]]
                up = table[nbr[b, SLOT[ox, oy, 1]], xs, :, 0:128]
                down = table[nbr[b, SLOT[ox, oy, -1]], xs, :, 384:512]
                return jnp.concatenate([table[t, xs], jnp.where(low, up, down)], axis=1)

            here = tile(0)
            shifts[0].append(pltpu.roll(jnp.where(row == 7, tile(-1), here), 1, 0))
            shifts[1].append(here)
            shifts[2].append(pltpu.roll(jnp.where(row == 0, tile(1), here), 7, 0))
        for c in range(3):
            pair_store(pad, c, xp * 8 * nb, shifts[c], slice(None))


def windows(nb, pad, a, c):
    rows = slice(8 * nb * a, 8 * nb * (a + 8))
    one = jnp.concatenate([pad[c, rows, 0:384], pad[c, rows, 512:640]], axis=1)
    two = jnp.concatenate([pad[c, rows, 256:640], pad[c, rows, 128:256]], axis=1)
    return one, two


def weight_matmuls(nb, pad, gt, packed):
    low = lax.broadcasted_iota(jnp.int32, (64, 128), 1) < 64
    for a in range(3):
        for c in range(3):
            one, two = windows(nb, pad, a, c)
            full = jnp.dot(gt[...], jnp.concatenate([one, two], axis=0), preferred_element_type=F32)

            def part(i, t):
                return full[64 * i : 64 * i + 64, 128 * t : 128 * t + 128]

            x0 = part(0, 3) + part(2, 0)
            x2 = part(1, 1) + part(3, 2)
            s02 = part(0, 0) + part(2, 1)
            s13 = part(1, 0) + part(3, 1)
            packed[0, 3 * a + c] = jnp.where(low, s02, x0) + pltpu.roll(s13, 64, 1)
            packed[1, 3 * a + c] = s02 + pltpu.roll(x2, 64, 1)


def forward(nb, pad, bands, mask, out):
    totals = [None, None]
    for a in range(3):
        for c in range(3):
            for w, rows in enumerate(windows(nb, pad, a, c)):
                term = jnp.dot(rows, bands[c, :, 256 * a : 256 * a + 256], preferred_element_type=F32)
                totals[w] = term if totals[w] is None else totals[w] + term
    for w in range(2):
        total = totals[w].reshape(8, nb, 8, 256)
        lanes = slice(256 * w, 256 * w + 256)
        for b in range(nb):
            out[b, :, :, lanes] = (total[:, b] * mask[b, :, :, lanes]).astype(BF16)


def fill_mask(nb, occ, mask):
    for b in range(nb):
        mask[b] = live_mask(occ[b])


def local_kernel(
    feat, grad, occ, band, got0, got1, got2, got3, nbr, out, inner, back, packed,
    mask, bands, gz, gt, dp, acc, table, pad,
):
    nb = feat.shape[0]
    cap = got0.shape[0]
    fill_mask(nb, occ, mask)
    build_bands(band, bands)
    fill_grads(nb, grad, mask, gz, gt)
    back_matmuls(nb, gz, bands, dp)
    scatter(nb, dp, nbr, acc)
    inner[...] = acc[:nb]
    for k in range(4):
        for j in range(cap):
            back[k, j] = acc[nb + k * cap + j].astype(BF16)
    for b in range(nb):
        table[b] = mask_feats(mask[b], feat[b])
    for k, got in enumerate((got0, got1, got2, got3)):
        for j in range(cap):
            table[nb + k * cap + j] = got[j].astype(F32)
    table[nb + 4 * cap] = jnp.zeros((8, 8, 512), F32)
    fill_padded(nb, table, nbr, pad)
    weight_matmuls(nb, pad, gt, packed)
    forward(nb, pad, bands, mask, out)


def final_kernel(inner, occ, got0, got1, got2, got3, send, out):
    nb, cap = inner.shape[0], got0.shape[0]
    for b in range(nb):
        total = inner[b]
        for k, got in enumerate((got0, got1, got2, got3)):
            for j in range(cap):
                total = total + jnp.where(send[0, k, j] == b, got[j].astype(F32), 0.0)
        out[b] = (total * live_mask(occ[b])).astype(BF16)


def on_device(features, grad_out, occupancy, weight, neighbours, send_rows):
    nb, cap = features.shape[0], send_rows.shape[2]
    slots = nb + 4 * cap + 1
    wide = 8 * nb
    params = pltpu.CompilerParams(vmem_limit_bytes=LIMIT)
    occ = (occupancy == 1).astype(BF16).reshape(nb, 64, 8)
    band = band_weights(weight)
    block = (8, 8, 512)
    outgoing = pl.pallas_call(
        outgoing_kernel,
        out_shape=jax.ShapeDtypeStruct((4, cap) + block, BF16),
        in_specs=[VMEM, VMEM, SMEM],
        out_specs=VMEM,
        compiler_params=params,
    )(features, occ, send_rows)
    got = [shifted(outgoing[k], "space", d) for k, d in enumerate(DISTANCES)]
    out, inner, back, packed = pl.pallas_call(
        local_kernel,
        out_shape=(
            jax.ShapeDtypeStruct((nb,) + block, BF16),
            jax.ShapeDtypeStruct((nb,) + block, F32),
            jax.ShapeDtypeStruct((4, cap) + block, BF16),
            jax.ShapeDtypeStruct((2, 9, 64, 128), F32),
        ),
        in_specs=[VMEM] * 8 + [SMEM],
        out_specs=(VMEM,) * 4,
        scratch_shapes=[
            pltpu.VMEM((nb,) + block, F32),
            pltpu.VMEM((3, 512, 768), BF16),
            pltpu.VMEM((12 * wide, 512), BF16),
            pltpu.VMEM((256, 16 * wide), BF16),
            pltpu.VMEM((3, 10, nb, 8, 640), F32),
            pltpu.VMEM((slots,) + block, F32),
            pltpu.VMEM((slots,) + block, F32),
            pltpu.VMEM((3, 10 * wide, 640), BF16),
        ],
        compiler_params=params,
    )(features, grad_out, occ, band, *got, neighbours)
    arrived = [shifted(back[k], "space", -d) for k, d in enumerate(DISTANCES)]
    feature_grad = pl.pallas_call(
        final_kernel,
        out_shape=jax.ShapeDtypeStruct((nb,) + block, BF16),
        in_specs=[VMEM] * 6 + [SMEM],
        out_specs=VMEM,
        compiler_params=params,
    )(inner, occ, *arrived, send_rows)
    scale = 1.0 / math.sqrt(lax.axis_size("space") * lax.axis_size("dp") * nb * 512)
    total = lax.psum(packed, ("space", "dp"))
    turned = jnp.swapaxes(total, 2, 3) * scale
    taps = jnp.stack([turned[0, :, 64:], turned[0, :, :64], turned[1, :, 64:]], axis=1)
    return out, feature_grad, taps.reshape(weight.shape)


def solution(mesh):
    whole = ("space", "dp")
    return jax.shard_map(
        on_device,
        mesh=mesh,
        in_specs=(
            P(whole, None, None, None),
            P(whole, None, None, None),
            P(whole, None),
            P(),
            P(whole, None),
            P(whole, None, None),
        ),
        out_specs=(P(whole, None, None, None), P(whole, None, None, None), P()),
        check_vma=False,
    )
```

```python
import functools
import math

import jax
import jax.numpy as jnp
from jax import lax
from jax.experimental import pallas as pl
from jax.experimental.pallas import tpu as pltpu
from jax.sharding import PartitionSpec as P

DISTANCES = (1, -1, 2, -2)
OFFSETS = [
    (step_x, step_y, step_z)
    for step_x in (-1, 0, 1)
    for step_y in (-1, 0, 1)
    for step_z in (-1, 0, 1)
    if (step_x, step_y, step_z) != (0, 0, 0)
]
SLOT = {offset: num for num, offset in enumerate(OFFSETS)}
PLANES = {-1: (7, 8, 0, 1), 0: (0, 8, 1, 9), 1: (0, 1, 9, 10)}
F32, BF16 = jnp.float32, jnp.bfloat16
VMEM = pl.BlockSpec(memory_space=pltpu.VMEM)
SMEM = pl.BlockSpec(memory_space=pltpu.SMEM)
LIMIT = 56 * 1024 * 1024


MESH = pl.DeviceIdType.MESH
TILES = 14


def greet(partners):
    barrier = pltpu.get_barrier_semaphore()
    for device in partners:
        pl.semaphore_signal(barrier, inc=1, device_id=device, device_id_type=MESH)


def greeted(count):
    pl.semaphore_wait(pltpu.get_barrier_semaphore(), count)


def remote(src, dst, send_sem, recv_sem, device):
    return pltpu.make_async_remote_copy(
        src_ref=src, dst_ref=dst, send_sem=send_sem, recv_sem=recv_sem,
        device_id=device, device_id_type=MESH,
    )


def band_weights(weight):
    channels = weight.shape[-1]
    zero_block = jnp.zeros((3, 3, channels, channels), weight.dtype)
    stacked = []
    for tap_in in range(4):
        parts = [
            weight[:, :, tap_in - out_pos] if 0 <= tap_in - out_pos <= 2 else zero_block
            for out_pos in range(2)
        ]
        stacked.append(jnp.concatenate(parts, axis=3))
    return jnp.stack(stacked, axis=2)


def live_mask(occ):
    spread = (
        lax.broadcasted_iota(jnp.int32, (8, 512), 1) // 64
        == lax.broadcasted_iota(jnp.int32, (8, 512), 0)
    ).astype(BF16)
    return jnp.dot(occ, spread, preferred_element_type=F32).reshape(8, 8, 512)


def mask_feats(mask, values):
    return jnp.where(mask > 0.5, values.astype(F32), 0.0)


def lend_kernel(n, feat, occ, send, got, held, send_sem, recv_sem):
    nb, cap = feat.shape[0], send.shape[2]
    here, core = lax.axis_index("space"), lax.axis_index("dp")
    partners = [(lax.rem(here + d + n, n), core) for d in DISTANCES]
    greet(partners)
    for k in range(4):
        for j in range(cap):
            row = jnp.minimum(send[0, k, j], nb - 1)
            held[k, j] = mask_feats(live_mask(occ[row]), feat[row]).astype(BF16)
        if k == 0:
            greeted(4)
        remote(held.at[k], got.at[k], send_sem.at[k], recv_sem.at[k], partners[k]).start()
    for k in range(4):
        remote(held.at[k], got.at[k], send_sem.at[k], recv_sem.at[k], partners[k]).wait()


def build_bands(band, bands):
    zero = jnp.zeros((64, 128), BF16)
    for a in range(3):
        for c in range(3):
            for k, r in enumerate((0, 1, 2, 3, 4, None, None, -1)):
                for j in range(2):
                    d = None if r is None else r - 2 * j
                    piece = zero if d is None or not -1 <= d <= 2 else band[a, c, d + 1]
                    bands[c, 64 * k : 64 * k + 64, 256 * a + 128 * j : 256 * a + 128 * j + 128] = piece


def pair_store(dst, lead, row0, tiles, lanes):
    for b in range(0, len(tiles), 2):
        both = jnp.concatenate([tiles[b], tiles[b + 1]], axis=0).astype(BF16)
        if lead is None:
            dst[row0 + 8 * b : row0 + 8 * b + 16, lanes] = both
        else:
            dst[lead, row0 + 8 * b : row0 + 8 * b + 16, lanes] = both


def fill_grads(nb, grad, mask, gz, gt):
    wide = 8 * nb
    for x in (0, 1, 10, 11):
        gz[x * wide : (x + 1) * wide] = jnp.zeros((wide, 512), BF16)
    for b in range(0, nb, 2):
        one = mask_feats(mask[b], grad[b])
        two = mask_feats(mask[b + 1], grad[b + 1])
        both = jnp.concatenate([one, two], axis=1).astype(BF16)
        for x in range(8):
            row = (x + 2) * wide + 8 * b
            gz[row : row + 16] = both[x]
    flat = gz[2 * wide : 10 * wide].astype(F32).T.astype(BF16)
    gt[:, : 8 * wide] = flat[:256]
    gt[:, 8 * wide :] = flat[256:]


def nt_dot(left, right):
    return lax.dot_general(left, right, (((1,), (1,)), ((), ())), preferred_element_type=F32)


def back_matmuls(nb, gz, bands, dp):
    wide = 8 * nb
    for c in range(3):
        parts = []
        for w in range(2):
            left = jnp.concatenate(
                [gz[wide * (2 - a) : wide * (12 - a), 256 * w : 256 * w + 256] for a in range(3)],
                axis=1,
            )
            parts.append(nt_dot(left, bands[c]).reshape(10, nb, 8, 512))
        one, two = parts
        dp[c, :, :, :, 0:128] = one[..., 0:128]
        dp[c, :, :, :, 128:256] = one[..., 128:256] + two[..., 384:512]
        dp[c, :, :, :, 256:384] = one[..., 256:384] + two[..., 0:128]
        dp[c, :, :, :, 384:512] = two[..., 128:256]
        dp[c, :, :, :, 512:640] = one[..., 384:512] + two[..., 256:384]


def scatter(nb, dp, nbr, acc):
    acc[...] = jnp.zeros(acc.shape, F32)
    for b in range(nb):
        for ox in (0, -1, 1):
            x0, x1, p0, p1 = PLANES[ox]
            n = p1 - p0
            row = lax.broadcasted_iota(jnp.int32, (n, 8, 640), 1)
            low = lax.broadcasted_iota(jnp.int32, (n, 8, 128), 2) < 64
            flat = (n * 8, 640)

            def turned(value, by):
                return pltpu.roll(value, by, 1)

            r0 = turned(dp[0, p0:p1, b], 7)
            r2 = turned(dp[2, p0:p1, b], 1)
            tiles = {
                0: dp[1, p0:p1, b] + jnp.where(row < 7, r0, 0.0) + jnp.where(row > 0, r2, 0.0),
                -1: jnp.where(row == 7, r0, 0.0),
                1: jnp.where(row == 0, r2, 0.0),
            }
            for oy in (0, -1, 1):
                tile = tiles[oy]
                t = b if (ox, oy) == (0, 0) else nbr[b, SLOT[ox, oy, 0]]
                acc[t, x0:x1] += tile[..., :512]
                halo = tile[..., 512:]
                acc[nbr[b, SLOT[ox, oy, 1]], x0:x1, :, 0:128] += jnp.where(low, halo, 0.0)
                acc[nbr[b, SLOT[ox, oy, -1]], x0:x1, :, 384:512] += jnp.where(low, 0.0, halo)


def fill_padded(nb, table, nbr, pad):
    row = lax.broadcasted_iota(jnp.int32, (8, 640), 0)
    low = lax.broadcasted_iota(jnp.int32, (8, 128), 1) < 64
    for xp in range(10):
        ox = -1 if xp == 0 else 1 if xp == 9 else 0
        xs = {-1: 7, 0: xp - 1, 1: 0}[ox]
        shifts = ([], [], [])
        for b in range(nb):

            def tile(oy):
                t = b if (ox, oy) == (0, 0) else nbr[b, SLOT[ox, oy, 0]]
                up = table[nbr[b, SLOT[ox, oy, 1]], xs, :, 0:128]
                down = table[nbr[b, SLOT[ox, oy, -1]], xs, :, 384:512]
                return jnp.concatenate([table[t, xs], jnp.where(low, up, down)], axis=1)

            here = tile(0)
            shifts[0].append(pltpu.roll(jnp.where(row == 7, tile(-1), here), 1, 0))
            shifts[1].append(here)
            shifts[2].append(pltpu.roll(jnp.where(row == 0, tile(1), here), 7, 0))
        for c in range(3):
            pair_store(pad, c, xp * 8 * nb, shifts[c], slice(None))


def windows(nb, pad, a, c):
    rows = slice(8 * nb * a, 8 * nb * (a + 8))
    one = jnp.concatenate([pad[c, rows, 0:384], pad[c, rows, 512:640]], axis=1)
    two = jnp.concatenate([pad[c, rows, 256:640], pad[c, rows, 128:256]], axis=1)
    return one, two


def weight_matmuls(nb, pad, gt, packed):
    odd = []
    low = lax.broadcasted_iota(jnp.int32, (64, 128), 1) < 64
    for a in range(3):
        for c in range(3):
            one, two = windows(nb, pad, a, c)
            full = jnp.dot(gt[...], jnp.concatenate([one, two], axis=0), preferred_element_type=F32)

            def part(i, t):
                return full[64 * i : 64 * i + 64, 128 * t : 128 * t + 128]

            x0 = part(0, 3) + part(2, 0)
            x2 = part(1, 1) + part(3, 2)
            s02 = part(0, 0) + part(2, 1)
            s13 = part(1, 0) + part(3, 1)
            packed[3 * a + c] = jnp.where(low, s02, x0) + pltpu.roll(s13, 64, 1)
            odd.append(s02 + pltpu.roll(x2, 64, 1))
    for q in range(5):
        left = pltpu.roll(odd[min(2 * q + 1, 8)], 64, 1)
        packed[9 + q] = jnp.where(low, left, odd[2 * q])


def forward(nb, pad, bands, mask, out):
    totals = [None, None]
    for a in range(3):
        for c in range(3):
            for w, rows in enumerate(windows(nb, pad, a, c)):
                term = jnp.dot(rows, bands[c, :, 256 * a : 256 * a + 256], preferred_element_type=F32)
                totals[w] = term if totals[w] is None else totals[w] + term
    for w in range(2):
        total = totals[w].reshape(8, nb, 8, 256)
        lanes = slice(256 * w, 256 * w + 256)
        for b in range(nb):
            out[b, :, :, lanes] = (total[:, b] * mask[b, :, :, lanes]).astype(BF16)


def fill_mask(nb, occ, mask):
    for b in range(nb):
        mask[b] = live_mask(occ[b])


def local_kernel(
    feat, grad, occ, band, got, nbr, out, inner, back, packed,
    mask, bands, gz, gt, dp, acc, table, pad,
):
    nb = feat.shape[0]
    cap = got.shape[1]
    fill_mask(nb, occ, mask)
    build_bands(band, bands)
    fill_grads(nb, grad, mask, gz, gt)
    back_matmuls(nb, gz, bands, dp)
    scatter(nb, dp, nbr, acc)
    inner[...] = acc[:nb]
    for k in range(4):
        for j in range(cap):
            back[k, j] = acc[nb + k * cap + j].astype(BF16)
    for b in range(nb):
        table[b] = mask_feats(mask[b], feat[b])
    for k in range(4):
        for j in range(cap):
            table[nb + k * cap + j] = got[k, j].astype(F32)
    table[nb + 4 * cap] = jnp.zeros((8, 8, 512), F32)
    fill_padded(nb, table, nbr, pad)
    weight_matmuls(nb, pad, gt, packed)
    forward(nb, pad, bands, mask, out)


def final_kernel(
    n, scale, inner, occ, back, packed, send, out, wout,
    got, swapped, half, shards, full, other,
    back_send, back_recv, rs_send, rs_recv, ag_send, ag_recv, core_send, core_recv,
):
    nb, cap = inner.shape[0], send.shape[2]
    here, core = lax.axis_index("space"), lax.axis_index("dp")
    twin = (here, 1 - core)
    rows, shard = packed.shape[0] // 2, half.shape[1]
    barrier = pltpu.get_barrier_semaphore()

    def hello(k, _):
        device = (lax.rem(here + k, n), core)
        pl.semaphore_signal(barrier, inc=1, device_id=device, device_id_type=MESH)
        return 0

    lax.fori_loop(1, n, hello, 0)
    pl.semaphore_signal(barrier, inc=1, device_id=twin, device_id_type=MESH)
    pl.semaphore_wait(barrier, n)

    theirs = pl.ds(pl.multiple_of((1 - core) * rows, 64), rows)
    mine = pl.ds(pl.multiple_of(core * rows, 64), rows)
    swap = remote(packed.at[theirs], swapped, core_send.at[0], core_recv.at[0], twin)
    swap.start()
    backs = [
        remote(back.at[k], got.at[k], back_send.at[k], back_recv.at[k], (lax.rem(here - d + n, n), core))
        for k, d in enumerate(DISTANCES)
    ]
    swap.wait()
    summed = packed[mine] + swapped[...]
    spare = n * shard - rows
    if spare:
        summed = jnp.concatenate([summed, jnp.zeros((spare, 128), F32)], axis=0)
    half[...] = summed.reshape(n, shard, 128)

    def reduce_copy(k):
        to = lax.rem(here + k, n)
        return remote(half.at[to], shards.at[k - 1], rs_send.at[k - 1], rs_recv.at[k - 1], (to, core))

    def gather_copy(k):
        to = lax.rem(here + k, n)
        return remote(full.at[here], full.at[here], ag_send.at[k - 1], ag_recv.at[k - 1], (to, core))

    def gather_arrival(k):
        slot = lax.rem(here - k + n, n)
        return remote(full.at[slot], full.at[slot], ag_send.at[k - 1], ag_recv.at[k - 1], (slot, core))

    def each(action):
        def body(k, _):
            action(k)
            return 0

        lax.fori_loop(1, n, body, 0)

    each(lambda k: reduce_copy(k).start())
    for copy in backs:
        copy.start()
    each(lambda k: reduce_copy(k).wait())
    total = half[here] + jnp.sum(shards[...], axis=0)
    full[here] = (total * scale).astype(BF16)
    each(lambda k: gather_copy(k).start())

    for copy in backs:
        copy.wait()
    for b in range(nb):
        total = inner[b]
        for k in range(4):
            for j in range(cap):
                total = total + jnp.where(send[0, k, j] == b, got[k, j].astype(F32), 0.0)
        out[b] = (total * live_mask(occ[b])).astype(BF16)

    each(lambda k: gather_copy(k).wait_send())
    each(lambda k: gather_arrival(k).wait_recv())
    swap = remote(full, other, core_send.at[1], core_recv.at[1], twin)
    swap.start()
    swap.wait()
    own = full[...].astype(F32).reshape(n * shard, 128)[:rows]
    far = other[...].astype(F32).reshape(n * shard, 128)[:rows]
    low = jnp.where(core == 0, own, far)
    high = jnp.where(core == 0, far, own)
    every = jnp.concatenate([low, high], axis=0)
    for q in range(TILES):
        turned = every[64 * q : 64 * q + 64].T
        if q < 9:
            wout[3 * q + 1] = turned[:64]
            wout[3 * q] = turned[64:]
        else:
            pair = 2 * (q - 9)
            wout[3 * pair + 2] = turned[64:]
            if pair + 1 < 9:
                wout[3 * pair + 5] = turned[:64]


def on_device(features, grad_out, occupancy, weight, neighbours, send_rows):
    nb, cap = features.shape[0], send_rows.shape[2]
    slots = nb + 4 * cap + 1
    wide = 8 * nb
    params = pltpu.CompilerParams(vmem_limit_bytes=LIMIT)
    occ = (occupancy == 1).astype(BF16).reshape(nb, 64, 8)
    band = band_weights(weight)
    block = (8, 8, 512)
    n = lax.axis_size("space")
    got = pl.pallas_call(
        functools.partial(lend_kernel, n),
        out_shape=jax.ShapeDtypeStruct((4, cap) + block, BF16),
        in_specs=[VMEM, VMEM, SMEM],
        out_specs=VMEM,
        scratch_shapes=[
            pltpu.VMEM((4, cap) + block, BF16),
            pltpu.SemaphoreType.DMA((4,)),
            pltpu.SemaphoreType.DMA((4,)),
        ],
        compiler_params=pltpu.CompilerParams(
            vmem_limit_bytes=LIMIT, collective_id=0, has_side_effects=True
        ),
    )(features, occ, send_rows)
    out, inner, back, packed = pl.pallas_call(
        local_kernel,
        out_shape=(
            jax.ShapeDtypeStruct((nb,) + block, BF16),
            jax.ShapeDtypeStruct((nb,) + block, F32),
            jax.ShapeDtypeStruct((4, cap) + block, BF16),
            jax.ShapeDtypeStruct((TILES, 64, 128), F32),
        ),
        in_specs=[VMEM] * 5 + [SMEM],
        out_specs=(VMEM,) * 4,
        scratch_shapes=[
            pltpu.VMEM((nb,) + block, F32),
            pltpu.VMEM((3, 512, 768), BF16),
            pltpu.VMEM((12 * wide, 512), BF16),
            pltpu.VMEM((256, 16 * wide), BF16),
            pltpu.VMEM((3, 10, nb, 8, 640), F32),
            pltpu.VMEM((slots,) + block, F32),
            pltpu.VMEM((slots,) + block, F32),
            pltpu.VMEM((3, 10 * wide, 640), BF16),
        ],
        compiler_params=params,
    )(features, grad_out, occ, band, got, neighbours)
    scale = 1.0 / math.sqrt(n * lax.axis_size("dp") * nb * 512)
    rows = TILES * 64 // 2
    shard = -(-rows // (16 * n)) * 16
    feature_grad, weight_grad = pl.pallas_call(
        functools.partial(final_kernel, n, scale),
        out_shape=(
            jax.ShapeDtypeStruct((nb,) + block, BF16),
            jax.ShapeDtypeStruct((27, 64, 64), F32),
        ),
        in_specs=[VMEM] * 4 + [SMEM],
        out_specs=(VMEM, VMEM),
        scratch_shapes=[
            pltpu.VMEM((4, cap) + block, BF16),
            pltpu.VMEM((rows, 128), F32),
            pltpu.VMEM((n, shard, 128), F32),
            pltpu.VMEM((n - 1, shard, 128), F32),
            pltpu.VMEM((n, shard, 128), BF16),
            pltpu.VMEM((n, shard, 128), BF16),
            pltpu.SemaphoreType.DMA((4,)),
            pltpu.SemaphoreType.DMA((4,)),
            pltpu.SemaphoreType.DMA((n - 1,)),
            pltpu.SemaphoreType.DMA((n - 1,)),
            pltpu.SemaphoreType.DMA((n - 1,)),
            pltpu.SemaphoreType.DMA((n - 1,)),
            pltpu.SemaphoreType.DMA((2,)),
            pltpu.SemaphoreType.DMA((2,)),
        ],
        compiler_params=pltpu.CompilerParams(
            vmem_limit_bytes=LIMIT, collective_id=1, has_side_effects=True
        ),
    )(inner, occ, back, packed.reshape(2 * rows, 128), send_rows)
    return out, feature_grad, weight_grad.reshape(weight.shape)


def solution(mesh):
    whole = ("space", "dp")
    return jax.shard_map(
        on_device,
        mesh=mesh,
        in_specs=(
            P(whole, None, None, None),
            P(whole, None, None, None),
            P(whole, None),
            P(),
            P(whole, None),
            P(whole, None, None),
        ),
        out_specs=(P(whole, None, None, None), P(whole, None, None, None), P()),
        check_vma=False,
    )
```

```python
import functools
import math

import jax
import jax.numpy as jnp
from jax import lax
from jax.experimental import pallas as pl
from jax.experimental.pallas import tpu as pltpu
from jax.sharding import PartitionSpec as P

DISTANCES = (1, -1, 2, -2)
OFFSETS = [
    (step_x, step_y, step_z)
    for step_x in (-1, 0, 1)
    for step_y in (-1, 0, 1)
    for step_z in (-1, 0, 1)
    if (step_x, step_y, step_z) != (0, 0, 0)
]
SLOT = {offset: num for num, offset in enumerate(OFFSETS)}
PLANES = {-1: (7, 8, 0, 1), 0: (0, 8, 1, 9), 1: (0, 1, 9, 10)}
F32, BF16 = jnp.float32, jnp.bfloat16
VMEM = pl.BlockSpec(memory_space=pltpu.VMEM)
SMEM = pl.BlockSpec(memory_space=pltpu.SMEM)
LIMIT = 56 * 1024 * 1024


MESH = pl.DeviceIdType.MESH
TILES = 14


def remote(src, dst, send_sem, recv_sem, device):
    return pltpu.make_async_remote_copy(
        src_ref=src, dst_ref=dst, send_sem=send_sem, recv_sem=recv_sem,
        device_id=device, device_id_type=MESH,
    )


def fill_mask(nb, occ, mask):
    voxel = lax.broadcasted_iota(jnp.int32, (64, 512), 1) // 8
    place = lax.broadcasted_iota(jnp.int32, (64, 512), 0)
    spread = (
        lax.broadcasted_iota(jnp.int32, (512, 512), 0) % 8
        == lax.broadcasted_iota(jnp.int32, (512, 512), 1) // 64
    ).astype(F32).astype(BF16)
    picks = [
        jnp.where((voxel == place) & (occ[b : b + 1] == 1), 1.0, 0.0).astype(BF16) for b in range(nb)
    ]
    full = jnp.dot(jnp.concatenate(picks, axis=0), spread, preferred_element_type=F32)
    mask[...] = full.reshape(nb, 8, 8, 512)


def mask_feats(mask, values):
    return jnp.where(mask > 0.5, values.astype(F32), 0.0)


def inside(n, place):
    return (place >= 0) & (place < n)


def lend_kernel(n, feat, occ, send, got, held, mask, send_sem, recv_sem):
    nb, cap = feat.shape[0], send.shape[0]
    here, core = lax.axis_index("space"), lax.axis_index("dp")
    barrier = pltpu.get_barrier_semaphore()
    for d in DISTANCES:

        @pl.when(inside(n, here + d))
        def _():
            pl.semaphore_signal(barrier, inc=1, device_id=(here + d, core), device_id_type=MESH)

    fill_mask(nb, occ, mask)
    for k in range(4):
        for j in range(cap):
            row = jnp.minimum(send[j, k], nb - 1)
            held[k, j] = mask_feats(mask[row], feat[row]).astype(BF16)
    pl.semaphore_wait(barrier, sum(jnp.where(inside(n, here + d), 1, 0) for d in DISTANCES))
    copies = exchange(n, here, core, held, got, send_sem, recv_sem, DISTANCES)
    copies[0]()
    copies[1]()


def exchange(n, here, core, src, dst, send_sem, recv_sem, distances):
    def copy(k):
        return remote(
            src.at[k], dst.at[k], send_sem.at[k], recv_sem.at[k], (here + distances[k], core)
        )

    def start():
        for k, d in enumerate(distances):

            @pl.when(inside(n, here + d))
            def _():
                copy(k).start()

    def finish():
        for k, d in enumerate(distances):

            @pl.when(inside(n, here + d))
            def _():
                copy(k).wait_send()

            @pl.when(inside(n, here - d))
            def _():
                copy(k).wait_recv()

            @pl.when(jnp.logical_not(inside(n, here - d)))
            def _():
                dst[k] = jnp.zeros(dst.shape[1:], dst.dtype)

    return start, finish


def build_bands(weight, bands):
    zero = jnp.zeros((64, 128), BF16)
    for a in range(3):
        for c in range(3):
            taps = [weight[9 * a + 3 * c + e] for e in range(3)]
            none = jnp.zeros((64, 64), BF16)
            pieces = [
                jnp.concatenate(pair, axis=1)
                for pair in zip(taps + [none], [none] + taps, strict=True)
            ]
            for k, r in enumerate((0, 1, 2, 3, 4, None, None, -1)):
                for j in range(2):
                    d = None if r is None else r - 2 * j
                    piece = zero if d is None or not -1 <= d <= 2 else pieces[d + 1]
                    bands[c, 64 * k : 64 * k + 64, 256 * a + 128 * j : 256 * a + 128 * j + 128] = piece


def pair_store(dst, lead, row0, tiles, lanes):
    for b in range(0, len(tiles), 2):
        both = jnp.concatenate([tiles[b], tiles[b + 1]], axis=0).astype(BF16)
        if lead is None:
            dst[row0 + 8 * b : row0 + 8 * b + 16, lanes] = both
        else:
            dst[lead, row0 + 8 * b : row0 + 8 * b + 16, lanes] = both


def fill_grads(nb, grad, mask, gz, gt):
    wide = 8 * nb
    for x in (0, 1, 10, 11):
        gz[x * wide : (x + 1) * wide] = jnp.zeros((wide, 512), BF16)
    for b in range(0, nb, 2):
        one = mask_feats(mask[b], grad[b])
        two = mask_feats(mask[b + 1], grad[b + 1])
        both = jnp.concatenate([one, two], axis=1).astype(BF16)
        for x in range(8):
            row = (x + 2) * wide + 8 * b
            gz[row : row + 16] = both[x]
    flat = gz[2 * wide : 10 * wide].astype(F32).T.astype(BF16)
    gt[:, : 8 * wide] = flat[:256]
    gt[:, 8 * wide :] = flat[256:]


def nt_dot(left, right):
    return lax.dot_general(left, right, (((1,), (1,)), ((), ())), preferred_element_type=F32)


def back_matmuls(nb, gz, bands, dp):
    wide = 8 * nb
    for c in range(3):
        parts = []
        for w in range(2):
            left = jnp.concatenate(
                [gz[wide * (2 - a) : wide * (12 - a), 256 * w : 256 * w + 256] for a in range(3)],
                axis=1,
            )
            parts.append(nt_dot(left, bands[c]).reshape(10, nb, 8, 512))
        one, two = parts
        dp[c, :, :, :, 0:128] = one[..., 0:128]
        dp[c, :, :, :, 128:256] = one[..., 128:256] + two[..., 384:512]
        dp[c, :, :, :, 256:384] = one[..., 256:384] + two[..., 0:128]
        dp[c, :, :, :, 384:512] = two[..., 128:256]
        dp[c, :, :, :, 512:640] = one[..., 384:512] + two[..., 256:384]


def scatter(nb, dp, nbr, acc):
    acc[...] = jnp.zeros(acc.shape, F32)
    for b in range(nb):
        for ox in (0, -1, 1):
            x0, x1, p0, p1 = PLANES[ox]
            n = p1 - p0
            row = lax.broadcasted_iota(jnp.int32, (n, 8, 640), 1)
            low = lax.broadcasted_iota(jnp.int32, (n, 8, 128), 2) < 64
            flat = (n * 8, 640)

            def turned(value, by):
                return pltpu.roll(value, by, 1)

            r0 = turned(dp[0, p0:p1, b], 7)
            r2 = turned(dp[2, p0:p1, b], 1)
            tiles = {
                0: dp[1, p0:p1, b] + jnp.where(row < 7, r0, 0.0) + jnp.where(row > 0, r2, 0.0),
                -1: jnp.where(row == 7, r0, 0.0),
                1: jnp.where(row == 0, r2, 0.0),
            }
            for oy in (0, -1, 1):
                tile = tiles[oy]
                t = b if (ox, oy) == (0, 0) else nbr[b, SLOT[ox, oy, 0]]
                acc[t, x0:x1] += tile[..., :512]
                halo = tile[..., 512:]
                acc[nbr[b, SLOT[ox, oy, 1]], x0:x1, :, 0:128] += jnp.where(low, halo, 0.0)
                acc[nbr[b, SLOT[ox, oy, -1]], x0:x1, :, 384:512] += jnp.where(low, 0.0, halo)


def fill_padded(nb, table, nbr, pad):
    row = lax.broadcasted_iota(jnp.int32, (8, 640), 0)
    low = lax.broadcasted_iota(jnp.int32, (8, 128), 1) < 64
    for xp in range(10):
        ox = -1 if xp == 0 else 1 if xp == 9 else 0
        xs = {-1: 7, 0: xp - 1, 1: 0}[ox]
        shifts = ([], [], [])
        for b in range(nb):

            def tile(oy):
                t = b if (ox, oy) == (0, 0) else nbr[b, SLOT[ox, oy, 0]]
                up = table[nbr[b, SLOT[ox, oy, 1]], xs, :, 0:128]
                down = table[nbr[b, SLOT[ox, oy, -1]], xs, :, 384:512]
                return jnp.concatenate([table[t, xs], jnp.where(low, up, down)], axis=1)

            here = tile(0)
            shifts[0].append(pltpu.roll(jnp.where(row == 7, tile(-1), here), 1, 0))
            shifts[1].append(here)
            shifts[2].append(pltpu.roll(jnp.where(row == 0, tile(1), here), 7, 0))
        for c in range(3):
            pair_store(pad, c, xp * 8 * nb, shifts[c], slice(None))


def windows(nb, pad, a, c):
    rows = slice(8 * nb * a, 8 * nb * (a + 8))
    one = jnp.concatenate([pad[c, rows, 0:384], pad[c, rows, 512:640]], axis=1)
    two = jnp.concatenate([pad[c, rows, 256:640], pad[c, rows, 128:256]], axis=1)
    return one, two


def weight_matmuls(nb, pad, gt, packed):
    odd = []
    low = lax.broadcasted_iota(jnp.int32, (64, 128), 1) < 64
    for a in range(3):
        for c in range(3):
            one, two = windows(nb, pad, a, c)
            full = jnp.dot(gt[...], jnp.concatenate([one, two], axis=0), preferred_element_type=F32)

            def part(i, t):
                return full[64 * i : 64 * i + 64, 128 * t : 128 * t + 128]

            x0 = part(0, 3) + part(2, 0)
            x2 = part(1, 1) + part(3, 2)
            s02 = part(0, 0) + part(2, 1)
            s13 = part(1, 0) + part(3, 1)
            packed[3 * a + c] = jnp.where(low, s02, x0) + pltpu.roll(s13, 64, 1)
            odd.append(s02 + pltpu.roll(x2, 64, 1))
    for q in range(5):
        left = pltpu.roll(odd[min(2 * q + 1, 8)], 64, 1)
        packed[9 + q] = jnp.where(low, left, odd[2 * q])


def forward(nb, pad, bands, mask, out):
    totals = [None, None]
    for a in range(3):
        for c in range(3):
            for w, rows in enumerate(windows(nb, pad, a, c)):
                term = jnp.dot(rows, bands[c, :, 256 * a : 256 * a + 256], preferred_element_type=F32)
                totals[w] = term if totals[w] is None else totals[w] + term
    for w in range(2):
        total = totals[w].reshape(8, nb, 8, 256)
        lanes = slice(256 * w, 256 * w + 256)
        for b in range(nb):
            out[b, :, :, lanes] = (total[:, b] * mask[b, :, :, lanes]).astype(BF16)


def local_kernel(
    feat, grad, occ, weight, got, nbr, out, inner, back, packed,
    mask, bands, gz, gt, dp, acc, table, pad,
):
    nb = feat.shape[0]
    cap = got.shape[1]
    fill_mask(nb, occ, mask)
    build_bands(weight, bands)
    fill_grads(nb, grad, mask, gz, gt)
    back_matmuls(nb, gz, bands, dp)
    scatter(nb, dp, nbr, acc)
    inner[...] = acc[:nb]
    for k in range(4):
        for j in range(cap):
            back[k, j] = acc[nb + k * cap + j].astype(BF16)
    for b in range(nb):
        table[b] = mask_feats(mask[b], feat[b])
    for k in range(4):
        for j in range(cap):
            table[nb + k * cap + j] = got[k, j].astype(F32)
    table[nb + 4 * cap] = jnp.zeros((8, 8, 512), F32)
    fill_padded(nb, table, nbr, pad)
    weight_matmuls(nb, pad, gt, packed)
    forward(nb, pad, bands, mask, out)


def final_kernel(
    n, scale, inner, occ, back, packed, send, out, wout,
    got, mask, swapped, half, shards, full, other,
    back_send, back_recv, rs_send, rs_recv, ag_send, ag_recv, core_send, core_recv,
):
    nb, cap = inner.shape[0], send.shape[0]
    here, core = lax.axis_index("space"), lax.axis_index("dp")
    twin = (here, 1 - core)
    rows, shard = packed.shape[0] // 2, half.shape[1]
    barrier = pltpu.get_barrier_semaphore()

    def hello(k, _):
        device = (lax.rem(here + k, n), core)
        pl.semaphore_signal(barrier, inc=1, device_id=device, device_id_type=MESH)
        return 0

    lax.fori_loop(1, n, hello, 0)
    pl.semaphore_signal(barrier, inc=1, device_id=twin, device_id_type=MESH)
    pl.semaphore_wait(barrier, n)

    theirs = pl.ds(pl.multiple_of((1 - core) * rows, 64), rows)
    mine = pl.ds(pl.multiple_of(core * rows, 64), rows)
    swap = remote(packed.at[theirs], swapped, core_send.at[0], core_recv.at[0], twin)
    swap.start()
    start_backs, finish_backs = exchange(
        n, here, core, back, got, back_send, back_recv, [-d for d in DISTANCES]
    )
    swap.wait()
    summed = packed[mine] + swapped[...]
    spare = n * shard - rows
    if spare:
        summed = jnp.concatenate([summed, jnp.zeros((spare, 128), F32)], axis=0)
    half[...] = summed.reshape(n, shard, 128)

    def reduce_copy(k):
        to = lax.rem(here + k, n)
        return remote(half.at[to], shards.at[k - 1], rs_send.at[k - 1], rs_recv.at[k - 1], (to, core))

    def gather_copy(k):
        to = lax.rem(here + k, n)
        return remote(full.at[here], full.at[here], ag_send.at[k - 1], ag_recv.at[k - 1], (to, core))

    def gather_arrival(k):
        slot = lax.rem(here - k + n, n)
        return remote(full.at[slot], full.at[slot], ag_send.at[k - 1], ag_recv.at[k - 1], (slot, core))

    def each(action):
        def body(k, _):
            action(k)
            return 0

        lax.fori_loop(1, n, body, 0)

    each(lambda k: reduce_copy(k).start())
    start_backs()
    each(lambda k: reduce_copy(k).wait())
    total = half[here] + jnp.sum(shards[...], axis=0)
    full[here] = (total * scale).astype(BF16)
    each(lambda k: gather_copy(k).start())

    fill_mask(nb, occ, mask)
    finish_backs()
    for b in range(nb):
        total = inner[b]
        for k in range(4):
            for j in range(cap):
                total = total + jnp.where(send[j, k] == b, got[k, j].astype(F32), 0.0)
        out[b] = (total * mask[b]).astype(BF16)

    each(lambda k: gather_copy(k).wait_send())
    each(lambda k: gather_arrival(k).wait_recv())
    swap = remote(full, other, core_send.at[1], core_recv.at[1], twin)
    swap.start()
    swap.wait()
    own = full[...].astype(F32).reshape(n * shard, 128)[:rows]
    far = other[...].astype(F32).reshape(n * shard, 128)[:rows]
    low = jnp.where(core == 0, own, far)
    high = jnp.where(core == 0, far, own)
    every = jnp.concatenate([low, high], axis=0)
    for q in range(TILES):
        turned = every[64 * q : 64 * q + 64].T
        if q < 9:
            wout[3 * q + 1] = turned[:64]
            wout[3 * q] = turned[64:]
        else:
            pair = 2 * (q - 9)
            wout[3 * pair + 2] = turned[64:]
            if pair + 1 < 9:
                wout[3 * pair + 5] = turned[:64]


def on_device(features, grad_out, occupancy, weight, neighbours, send_rows):
    nb, cap = features.shape[0], send_rows.shape[2]
    slots = nb + 4 * cap + 1
    wide = 8 * nb
    params = pltpu.CompilerParams(vmem_limit_bytes=LIMIT)
    occ = occupancy
    send_rows = send_rows.reshape(4, cap).T
    block = (8, 8, 512)
    n = lax.axis_size("space")
    got = pl.pallas_call(
        functools.partial(lend_kernel, n),
        out_shape=jax.ShapeDtypeStruct((4, cap) + block, BF16),
        in_specs=[VMEM, VMEM, SMEM],
        out_specs=VMEM,
        scratch_shapes=[
            pltpu.VMEM((4, cap) + block, BF16),
            pltpu.VMEM((nb,) + block, F32),
            pltpu.SemaphoreType.DMA((4,)),
            pltpu.SemaphoreType.DMA((4,)),
        ],
        compiler_params=pltpu.CompilerParams(
            vmem_limit_bytes=LIMIT, collective_id=0, has_side_effects=True
        ),
    )(features, occ, send_rows)
    out, inner, back, packed = pl.pallas_call(
        local_kernel,
        out_shape=(
            jax.ShapeDtypeStruct((nb,) + block, BF16),
            jax.ShapeDtypeStruct((nb,) + block, F32),
            jax.ShapeDtypeStruct((4, cap) + block, BF16),
            jax.ShapeDtypeStruct((TILES, 64, 128), F32),
        ),
        in_specs=[VMEM] * 5 + [SMEM],
        out_specs=(VMEM,) * 4,
        scratch_shapes=[
            pltpu.VMEM((nb,) + block, F32),
            pltpu.VMEM((3, 512, 768), BF16),
            pltpu.VMEM((12 * wide, 512), BF16),
            pltpu.VMEM((256, 16 * wide), BF16),
            pltpu.VMEM((3, 10, nb, 8, 640), F32),
            pltpu.VMEM((slots,) + block, F32),
            pltpu.VMEM((slots,) + block, F32),
            pltpu.VMEM((3, 10 * wide, 640), BF16),
        ],
        compiler_params=params,
    )(features, grad_out, occ, weight.reshape(27, 64, 64), got, neighbours)
    scale = 1.0 / math.sqrt(n * lax.axis_size("dp") * nb * 512)
    rows = TILES * 64 // 2
    shard = -(-rows // (16 * n)) * 16
    feature_grad, weight_grad = pl.pallas_call(
        functools.partial(final_kernel, n, scale),
        out_shape=(
            jax.ShapeDtypeStruct((nb,) + block, BF16),
            jax.ShapeDtypeStruct((27, 64, 64), F32),
        ),
        in_specs=[VMEM] * 4 + [SMEM],
        out_specs=(VMEM, VMEM),
        scratch_shapes=[
            pltpu.VMEM((4, cap) + block, BF16),
            pltpu.VMEM((nb,) + block, F32),
            pltpu.VMEM((rows, 128), F32),
            pltpu.VMEM((n, shard, 128), F32),
            pltpu.VMEM((n - 1, shard, 128), F32),
            pltpu.VMEM((n, shard, 128), BF16),
            pltpu.VMEM((n, shard, 128), BF16),
            pltpu.SemaphoreType.DMA((4,)),
            pltpu.SemaphoreType.DMA((4,)),
            pltpu.SemaphoreType.DMA((n - 1,)),
            pltpu.SemaphoreType.DMA((n - 1,)),
            pltpu.SemaphoreType.DMA((n - 1,)),
            pltpu.SemaphoreType.DMA((n - 1,)),
            pltpu.SemaphoreType.DMA((2,)),
            pltpu.SemaphoreType.DMA((2,)),
        ],
        compiler_params=pltpu.CompilerParams(
            vmem_limit_bytes=LIMIT, collective_id=1, has_side_effects=True
        ),
    )(inner, occ, back, packed.reshape(2 * rows, 128), send_rows)
    return out, feature_grad, weight_grad.reshape(weight.shape)


def solution(mesh):
    whole = ("space", "dp")
    return jax.shard_map(
        on_device,
        mesh=mesh,
        in_specs=(
            P(whole, None, None, None),
            P(whole, None, None, None),
            P(whole, None),
            P(),
            P(whole, None),
            P(whole, None, None),
        ),
        out_specs=(P(whole, None, None, None), P(whole, None, None, None), P()),
        check_vma=False,
    )
```
